768 devices in a mesh: slab: 96 (over x, z, core), view: 8 (over y).
Axes of the slice: x: 4, y: 8, z: 12, core: 2. Of those that a mesh axis runs over, the one named last changes fastest.
Arguments:
- residual: bfloat16 [768, 192, 2, 128], P(('view', 'slab')), may hold values from -96 to 96
- route_list: int32 [768, 96, 2], P(('view', 'slab')), may hold values from -1 to 191, as said below
- tile_offsets: int32 [768], replicated, may hold values from 0 to 15
- view_geometry: float32 [4, 768], replicated, may hold values from 0 to 1
- line_coords: float32 [2, 1536, 128], P(None, 'slab'), may hold values from 0 to 1
- occupied: int32 [96, 8], P('slab'), may hold values from -1 to 15, as said below
- volume: float32 [1536, 128, 128], P('slab', 'view'), may hold values from -0.9 to 0.9
Outputs:
- new_volume: float32 [1536, 128, 128], P('slab', 'view')
The draws below stay inside these ranges and needn't reach their ends.
Inputs may be any that keep to these rules, and one draw needn't show every extreme that they name: route_list[a, s, 0] is a block of view a's window that meets slab s; route_list[a, s, 1] is the block after it, or -1 where only one block meets the slab. Slab 96 - 1 receives two blocks from every view. The first entries of occupied[s] (one or more) are distinct bricks of slab s, numbered 0 to 15; the remaining entries are -1. Some slab lists 8 bricks, and some slab lists brick 16 - 1.
All inputs are finite; a program needn't handle non-finite values.
Results may differ from the reference program's by a relative error of at most 0.0034.
Values may be sent and summed in bfloat16 or wider, within the bound.
A program may use at most 32 MiB of HBM per device.

```python
import jax
import jax.numpy as jnp
from jax import lax

COLS = 128
TROWS = 2
CAP = 2
BRICKS = 16
MAXB = 8
BR = 128
NBLK = 192
VIEWS = 768
LINES = 1536
N_SLAB = 96


def draw_route_list(key, part):
    key = jax.random.fold_in(key, 11)
    key_shift, key_keep, key_rate = jax.random.split(key, 3)
    view_ids = jnp.arange(VIEWS, dtype=jnp.int32)[:, None]
    slab_ids = jnp.arange(N_SLAB, dtype=jnp.int32)[None, :]
    shifts = jax.random.randint(key_shift, (VIEWS, 1), -1, 2)
    shifts = jnp.where(view_ids == 0, 0, shifts)
    leading = jnp.clip(2 * slab_ids + shifts, 0, NBLK - 2)
    run_count = (VIEWS + 15) // 16
    rates = jax.random.randint(key_rate, (1, N_SLAB), 2, 20)
    votes = jax.random.randint(key_keep, (run_count, N_SLAB), 0, 20)
    run_keep = votes < rates
    keeping = run_keep[view_ids[:, 0] // 16]
    keeping = keeping | (slab_ids == N_SLAB - 1)
    keeping = keeping & jnp.logical_not((view_ids == 1) & (slab_ids == 0))
    trailing = jnp.where(keeping, leading + 1, -1)
    return jnp.stack([leading, trailing], axis=-1).astype(jnp.int32)


def draw_occupied(key, part):
    key = jax.random.fold_in(key, 23)
    key_perm, key_count, key_full = jax.random.split(key, 3)
    orders = jax.vmap(lambda single: jax.random.permutation(single, BRICKS))(jax.random.split(key_perm, N_SLAB))
    fullest = jax.random.randint(key_full, (), 0, N_SLAB)
    slab_ids = jnp.arange(N_SLAB, dtype=jnp.int32)
    rotated = (orders - orders[:, :1] + (BRICKS - 1)) % BRICKS
    orders = jnp.where((slab_ids == fullest)[:, None], rotated, orders)
    picks = orders[:, :MAXB]
    counts = jax.random.randint(key_count, (N_SLAB,), 1, MAXB // 2 + 2)
    counts = jnp.minimum(counts, MAXB)
    counts = jnp.where(slab_ids == fullest, MAXB, counts)
    counts = jnp.where(slab_ids == (fullest + 1) % N_SLAB, 1, counts)
    slots = jnp.arange(MAXB, dtype=jnp.int32)[None, :]
    return jnp.where(slots < counts[:, None], picks, -1).astype(jnp.int32)


def plant(entries, key, smallest, top_value):
    spot = [jax.random.randint(jax.random.fold_in(key, axis), (), 0, length) for axis, length in enumerate(entries.shape)]
    longest = entries.shape.index(max(entries.shape))
    next_to = spot[:longest] + [(spot[longest] + 1) % entries.shape[longest]] + spot[longest + 1:]
    return entries.at[tuple(spot)].set(smallest).at[tuple(next_to)].set(top_value)


def steps_of(key, shape, cuts, least, largest):
    level = 1.0
    for dim, shards_of in cuts:
        steps = jax.random.uniform(jax.random.fold_in(jax.random.fold_in(key, 6), dim), (shards_of,), jnp.float32, least / len(cuts), largest / len(cuts))
        level = level * jnp.repeat(jnp.exp(steps), shape[dim] // shards_of).reshape((-1,) + (1,) * (len(shape) - 1 - dim))
    return level


def noise(own_key, extent, spread, bound, pieces=(), kind=jnp.bfloat16):
    array = spread * jax.random.normal(own_key, extent, jnp.float32)
    if pieces:
        array = array * steps_of(own_key, extent, pieces, -0.22, 0.18)
    return jnp.clip(array, -bound, bound).astype(kind)


def setup_inputs(seed: int = 0) -> dict:
    splits = jax.random.split(jax.random.key(seed), 8)
    return {
        "residual": noise(splits[0], (VIEWS, NBLK, TROWS, COLS), 16.0, 96.0, ((0, 768),)),
        "route_list": draw_route_list(jax.random.fold_in(splits[7], 71), 0),
        "tile_offsets": plant(jax.random.randint(splits[2], (VIEWS,), 0, COLS // 8), jax.random.fold_in(splits[2], 1), 0, (COLS // 8) - 1).astype(jnp.int32),
        "view_geometry": jnp.clip(jax.random.uniform(splits[3], (4, VIEWS), jnp.float32, 0.0, 1.0), 0.0, 1.0),
        "line_coords": jnp.clip(1.0 * jax.random.uniform(splits[4], (2, LINES, BR), jnp.float32) ** steps_of(splits[4], (2, LINES, BR), ((1, 96),), -0.2, 0.2), 0.0, 1.0),
        "occupied": draw_occupied(jax.random.fold_in(splits[7], 71), 0),
        "volume": noise(splits[6], (LINES, BR, COLS), 0.15, 0.9, ((0, 96), (1, 8)), jnp.float32),
    }


relaxation = 0.9
damping = 0.1


def column_table(scales, offsets, columns):
    slopes = 0.8 + 0.05 * scales
    centre = offsets.astype(jnp.float32)[:, None] + slopes[:, None] * jnp.arange(columns, dtype=jnp.float32)[None, :]
    detector = jnp.arange(columns, dtype=jnp.float32)
    return jnp.maximum(0.0, 1.0 - jnp.abs(detector[None, :, None] - centre[:, None, :])).astype(jnp.bfloat16)


def line_hats(heights, depths, geometry, row_total):
    centre = 1.25 + 0.5 * geometry[0]
    tilt_rate = 0.6 + 0.6 * geometry[1]
    sweeps = 1.2 * geometry[2] - 0.6
    position = centre + tilt_rate * (heights[:, None] - 1.5) + sweeps * depths[:, None]
    levels = jnp.arange(row_total, dtype=jnp.float32)
    weight = jnp.maximum(0.0, 1.0 - jnp.abs(position[:, :, None] - levels))
    return weight.reshape(weight.shape[0], -1).astype(jnp.bfloat16)


def reference(residual, route_list, tile_offsets, view_geometry, line_coords, occupied, volume):
    tables = column_table(view_geometry[3], tile_offsets, COLS)
    view_index = jnp.arange(VIEWS, dtype=jnp.int32)[:, None]
    row_total = CAP * TROWS

    def one_slab(slab_id):
        listed = lax.dynamic_index_in_dim(route_list, slab_id, 1, keepdims=False)
        present = listed >= 0
        blocks = residual[view_index, jnp.maximum(listed, 0)]
        blocks = jnp.where(present[:, :, None, None], blocks, jnp.zeros((), jnp.bfloat16))
        stacked = blocks.reshape(VIEWS, row_total, COLS)
        row_marks = jnp.repeat(present, TROWS, axis=1).astype(jnp.bfloat16)
        projected = jnp.einsum("vjc,vcx->vjx", stacked.astype(jnp.float32), tables.astype(jnp.float32)).astype(jnp.bfloat16)
        flat_rows = projected.reshape(VIEWS * row_total, COLS)
        mark_flat = row_marks.reshape(-1)
        chosen = lax.dynamic_index_in_dim(occupied, slab_id, 0, keepdims=False)
        coords = lax.dynamic_slice_in_dim(line_coords, slab_id * BRICKS, BRICKS, 1)

        def one_brick(brick_id):
            picked = lax.dynamic_index_in_dim(coords, jnp.maximum(brick_id, 0), 1, keepdims=False)
            weights = line_hats(3.0 * picked[0], picked[1] - 0.5, view_geometry, row_total)
            numerator = jnp.dot(weights, flat_rows, preferred_element_type=jnp.float32)
            ray_sum = jnp.dot(weights, mark_flat, preferred_element_type=jnp.float32)
            return relaxation * numerator / (ray_sum[:, None] + damping * VIEWS)

        updates = lax.map(one_brick, chosen)
        onehot = (chosen[None, :] == jnp.arange(BRICKS, dtype=jnp.int32)[:, None]).astype(jnp.float32)
        brick_add = jnp.einsum("bm,mrc->brc", onehot, updates, precision=lax.Precision.HIGHEST)
        return lax.dynamic_slice_in_dim(volume, slab_id * BRICKS, BRICKS, 0) + brick_add

    all_slabs = lax.map(one_slab, jnp.arange(N_SLAB, dtype=jnp.int32))
    return all_slabs.reshape(LINES, BR, COLS)
```

```python
import jax
import jax.numpy as jnp
from jax import lax
from jax.experimental import pallas as pl
from jax.experimental.pallas import tpu as pltpu
from jax.sharding import PartitionSpec as P

MESH = pl.DeviceIdType.MESH
F32 = jnp.float32
BF16 = jnp.bfloat16

NS = 96
NV = 8
VIEWS = 768
ROWS = 8
K = NS * ROWS
MB = 8
SHARE = 16
CHUNK = MB * SHARE
MSG = CHUNK + 16
RELAX = 0.9
SHIFT = 0.1 * VIEWS


def iota(shape, dim):
    return lax.broadcasted_iota(jnp.int32, shape, dim)


def drain(ref, sem):
    pltpu.make_async_copy(ref, ref, sem).wait()


def body(
    offs, occ, res, route, geo, lines, vol, out,
    snd, rcv, wgt, part, got, upd, ss, rs, ss2, rs2,
):
    s = lax.axis_index("slab")
    y = lax.axis_index("view")
    view = y * NS + s

    bar = pltpu.get_barrier_semaphore()

    def greet_slab(i, c):
        p = lax.rem(s + i, NS)
        pl.semaphore_signal(bar, inc=1, device_id=(p, y), device_id_type=MESH)
        return c

    lax.fori_loop(1, NS, greet_slab, 0)
    for d in range(1, NV):
        pl.semaphore_signal(bar, inc=1, device_id=(s, lax.rem(y + d, NV)), device_id_type=MESH)

    g = geo[...]
    lane = iota((4, VIEWS), 1)
    mine = jnp.sum(jnp.where(lane == view, g, 0.0), axis=1, keepdims=True)
    slope = 0.8 + 0.05 * mine[3:4, :]
    off = offs[view].astype(F32)
    col = iota((128, 128), 0).astype(F32)
    xs = iota((128, 128), 1).astype(F32)
    table = jnp.maximum(0.0, 1.0 - jnp.abs(col - (off + slope * xs))).astype(BF16)
    proj = jnp.dot(res[...], table, preferred_element_type=F32).astype(BF16)

    listed = route[0].astype(F32).astype(BF16)
    rr = iota((K, NS), 0)
    owner = (rr >> 3) == iota((K, NS), 1)
    spread = lax.dot_general(
        owner.astype(F32).astype(BF16), listed, (((1,), (1,)), ((), ())), preferred_element_type=F32
    )
    q = iota((K, 1), 0) & 7
    block = jnp.where((q & 2) == 0, spread[:, 0:1], spread[:, 1:2])
    want = jnp.where(q < 4, 2.0 * block + (q & 1).astype(F32), -1.0)
    pick = (iota((K, 384), 1).astype(F32) == want).astype(F32).astype(BF16)
    tile = jnp.dot(pick, proj, preferred_element_type=F32)
    mark = jnp.where((q >= 4) & (block >= 0.0), 1.0, 0.0)
    snd[...] = (tile + mark).astype(BF16).reshape(NS, ROWS, 128)

    pl.semaphore_wait(bar, NS - 1 + NV - 1)

    def send(i, c):
        p = lax.rem(s + i, NS)
        pltpu.make_async_remote_copy(
            src_ref=snd.at[p], dst_ref=rcv.at[s], send_sem=ss, recv_sem=rs,
            device_id=(p, y), device_id_type=MESH,
        ).start()
        return c

    lax.fori_loop(1, NS, send, 0)

    g1 = g.astype(BF16)
    r1 = g - g1.astype(F32)
    g2 = r1.astype(BF16)
    g3 = (r1 - g2.astype(F32)).astype(BF16)
    sel = (iota((VIEWS, K), 0) - y * NS) == (iota((VIEWS, K), 1) >> 3)
    sel = sel.astype(F32).astype(BF16)
    gg = (
        jnp.dot(g1, sel, preferred_element_type=F32)
        + jnp.dot(g2, sel, preferred_element_type=F32)
        + jnp.dot(g3, sel, preferred_element_type=F32)
    )
    centre = 1.25 + 0.5 * gg[0:1]
    tilt = 0.6 + 0.6 * gg[1:2]
    sweep = 1.2 * gg[2:3] - 0.6
    level = (iota((1, K), 1) & 3).astype(F32)
    hs = []
    ds = []
    for m in range(MB):
        brick = jnp.maximum(occ[0, m], 0)
        hs.append(3.0 * lines[0, pl.ds(brick, 1), :] - 1.5)
        ds.append(lines[1, pl.ds(brick, 1), :] - 0.5)
    hd = jnp.concatenate(hs + ds + [jnp.zeros((112, 128), F32)], axis=0)
    hdt = hd.T
    for d in range(NV):
        for m in range(MB):
            h = hdt[d * SHARE:(d + 1) * SHARE, m:m + 1]
            e = hdt[d * SHARE:(d + 1) * SHARE, MB + m:MB + m + 1]
            pos = centre + tilt * h + sweep * e
            w = jnp.maximum(0.0, 1.0 - jnp.abs(pos - level))
            wgt[pl.ds(d * CHUNK + m * SHARE, SHARE), :] = w.astype(BF16)

    drain(rcv.at[pl.ds(0, NS - 1)], rs)
    rcv[pl.ds(s, 1)] = snd[pl.ds(s, 1)]

    rows = rcv[...].reshape(K, 128)
    tiled = (iota((K, 128), 0) & 7) < 4
    zero = jnp.zeros((K, 128), BF16)
    both = jnp.concatenate([jnp.where(tiled, rows, zero), jnp.where(tiled, zero, rows)], axis=1)
    diag = iota((128, 128), 0) == iota((128, 128), 1)

    def chunk(d):
        r = jnp.dot(wgt[pl.ds(pl.multiple_of(d * CHUNK, CHUNK), CHUNK), :], both, preferred_element_type=F32)
        ray = jnp.sum(jnp.where(diag, r[:, 128:], 0.0), axis=0, keepdims=True)
        return r[:, :128], ray

    for d in (4, 3, 5, 2, 6, 1, 7):
        t = lax.rem(y + d, NV)
        num, ray = chunk(t)
        hi = ray.astype(BF16)
        lo = (ray - hi.astype(F32)).astype(BF16)
        part[t, 0:CHUNK, :] = num.astype(BF16)
        rowid = iota((16, 128), 0)
        hilo = jnp.where(rowid == 0, hi.astype(F32), jnp.where(rowid == 1, lo.astype(F32), 0.0))
        part[t, CHUNK:MSG, :] = hilo.astype(BF16)
        pltpu.make_async_remote_copy(
            src_ref=part.at[t], dst_ref=got.at[y], send_sem=ss2, recv_sem=rs2,
            device_id=(s, t), device_id_type=MESH,
        ).start()
    num, ray = chunk(y)
    got[pl.ds(y, 1)] = jnp.zeros((1, MSG, 128), BF16)
    drain(snd.at[pl.ds(0, NS - 1)], ss)
    drain(got.at[pl.ds(0, NV - 1)], rs2)
    for v in range(NV):
        num = num + got[v, 0:CHUNK, :].astype(F32)
        tail = got[v, CHUNK:MSG, :].astype(F32)
        ray = ray + (tail[0:1] + tail[1:2])
    rayc = jnp.broadcast_to(ray, (128, 128)).T
    new = RELAX * num / (rayc + SHIFT)
    upd[0:MB] = new.reshape(MB, SHARE, 128)
    upd[MB:MB + 1] = jnp.zeros((1, SHARE, 128), F32)
    for b in range(16):
        slot = jnp.int32(MB)
        for m in range(MB):
            slot = jnp.where(occ[0, m] == b, m, slot)
        out[b] = vol[b] + upd[slot]
    drain(part.at[pl.ds(0, NV - 1)], ss2)


def per_device(residual, route_list, tile_offsets, view_geometry, line_coords, occupied, volume):
    vm = pl.BlockSpec(memory_space=pltpu.VMEM)
    sm = pl.BlockSpec(memory_space=pltpu.SMEM)
    return pl.pallas_call(
        body,
        out_shape=jax.ShapeDtypeStruct(volume.shape, F32),
        in_specs=[sm, sm, vm, vm, vm, vm, vm],
        out_specs=vm,
        scratch_shapes=[
            pltpu.VMEM((NS, ROWS, 128), BF16),
            pltpu.VMEM((NS, ROWS, 128), BF16),
            pltpu.VMEM((NV * CHUNK, K), BF16),
            pltpu.VMEM((NV, MSG, 128), BF16),
            pltpu.VMEM((NV, MSG, 128), BF16),
            pltpu.VMEM((MB + 1, SHARE, 128), F32),
            pltpu.SemaphoreType.DMA,
            pltpu.SemaphoreType.DMA,
            pltpu.SemaphoreType.DMA,
            pltpu.SemaphoreType.DMA,
        ],
        compiler_params=pltpu.CompilerParams(
            collective_id=0, has_side_effects=True, vmem_limit_bytes=48 << 20
        ),
    )(
        tile_offsets, occupied, residual.reshape(384, 128), jnp.swapaxes(route_list, 1, 2), view_geometry,
        line_coords, volume,
    )


def solution(mesh):
    placed = (
        P(("view", "slab"), None, None, None),
        P(("view", "slab"), None, None),
        P(),
        P(),
        P(None, "slab", None),
        P("slab", None),
        P("slab", "view", None),
    )
    return jax.shard_map(
        per_device, mesh=mesh, in_specs=placed, out_specs=P("slab", "view", None), check_vma=False
    )
```

```python
import jax
import jax.numpy as jnp
from jax import lax
from jax.experimental import pallas as pl
from jax.experimental.pallas import tpu as pltpu
from jax.sharding import PartitionSpec as P

MESH = pl.DeviceIdType.MESH
F32 = jnp.float32
BF16 = jnp.bfloat16

NS = 96
NV = 8
VIEWS = 768
ROWS = 4
K = NS * ROWS
MB = 8
SHARE = 16
CHUNK = MB * SHARE
MSG = CHUNK + 16
RELAX = 0.9
SHIFT = 0.1 * VIEWS


def iota(shape, dim):
    return lax.broadcasted_iota(jnp.int32, shape, dim)


def drain(ref, sem):
    pltpu.make_async_copy(ref, ref, sem).wait()


def ring(v, step, n):
    t = v + step
    return jnp.where(t >= n, t - n, t)


def peers(s, act):
    x = s // 24
    z = (s - 24 * x) >> 1
    c = s & 1
    bases = [24 * ((x + dx) & 3) + (c ^ dc) for dx in (2, 1, 3, 0) for dc in (1, 0)]

    def column(i, carry):
        dz = jnp.where(i >= 6, i - 5, i + 6)
        t = 2 * ring(z, dz, 12)
        for base in bases:
            act(base + t)
        return carry

    lax.fori_loop(0, 11, column, 0)
    for base in bases[:-1]:
        act(base + 2 * z)


def body(
    offs_h, occ_h, res_h, route_h, geo_h, lines_h, vol_h, out,
    offs, occ, res, route, geo, lines, vol,
    snd, rcv, msnd, mrcv, wgt, part, got, upd, ins, ss, rs, ms, mr, ss2, rs2,
):
    s = lax.axis_index("slab")
    y = lax.axis_index("view")
    view = y * NS + s

    fetch = [
        pltpu.make_async_copy(h, v, ins.at[i])
        for i, (h, v) in enumerate(
            [
                (res_h, res), (route_h, route), (geo_h, geo), (offs_h, offs),
                (occ_h, occ), (lines_h, lines), (vol_h, vol),
            ]
        )
    ]
    for f in fetch:
        f.start()

    bar = pltpu.get_barrier_semaphore()

    def greet(p):
        pl.semaphore_signal(bar, inc=1, device_id=(p, y), device_id_type=MESH)

    peers(s, greet)
    for d in range(1, NV):
        pl.semaphore_signal(bar, inc=1, device_id=(s, (y + d) & 7), device_id_type=MESH)

    for f in fetch[:4]:
        f.wait()
    g = geo[...]
    lane = iota((4, VIEWS), 1)
    mine = jnp.sum(jnp.where(lane == view, g, 0.0), axis=1, keepdims=True)
    slope = 0.8 + 0.05 * mine[3:4, :]
    off = offs[view].astype(F32)
    col = iota((128, 128), 0).astype(F32)
    xs = iota((128, 128), 1).astype(F32)
    table = jnp.maximum(0.0, 1.0 - jnp.abs(col - (off + slope * xs))).astype(BF16)
    proj = jnp.dot(res[...], table, preferred_element_type=F32).astype(BF16)

    blocks = route[0].astype(F32)
    listed = blocks.astype(BF16)
    owner = (iota((K, NS), 0) >> 2) == iota((K, NS), 1)
    spread = lax.dot_general(
        owner.astype(F32).astype(BF16), listed, (((1,), (1,)), ((), ())), preferred_element_type=F32
    )
    q = iota((K, 1), 0) & 3
    block = jnp.where(q < 2, spread[:, 0:1], spread[:, 1:2])
    want = 2.0 * block + (q & 1).astype(F32)
    pick = (iota((K, 384), 1).astype(F32) == want).astype(F32).astype(BF16)
    tile = jnp.dot(pick, proj, preferred_element_type=F32)
    snd[...] = tile.astype(BF16).reshape(NS, ROWS, 128)
    flags = jnp.where(blocks >= 0.0, 1.0, 0.0)
    flags = jnp.concatenate([flags, jnp.zeros((2, 128 - NS), F32)], axis=1)
    msnd[...] = flags.astype(BF16).reshape(1, 2, 128)

    pl.semaphore_wait(bar, NS - 1 + NV - 1)

    def send(p):
        pltpu.make_async_remote_copy(
            src_ref=msnd.at[0], dst_ref=mrcv.at[s], send_sem=ms, recv_sem=mr,
            device_id=(p, y), device_id_type=MESH,
        ).start()
        pltpu.make_async_remote_copy(
            src_ref=snd.at[p], dst_ref=rcv.at[s], send_sem=ss, recv_sem=rs,
            device_id=(p, y), device_id_type=MESH,
        ).start()

    peers(s, send)

    for f in fetch[4:6]:
        f.wait()
    g1 = g.astype(BF16)
    r1 = g - g1.astype(F32)
    g2 = r1.astype(BF16)
    g3 = (r1 - g2.astype(F32)).astype(BF16)
    sel = (iota((VIEWS, K), 0) - y * NS) == (iota((VIEWS, K), 1) >> 2)
    sel = sel.astype(F32).astype(BF16)
    gg = (
        jnp.dot(g1, sel, preferred_element_type=F32)
        + jnp.dot(g2, sel, preferred_element_type=F32)
        + jnp.dot(g3, sel, preferred_element_type=F32)
    )
    centre = 1.25 + 0.5 * gg[0:1]
    tilt = 0.6 + 0.6 * gg[1:2]
    sweep = 1.2 * gg[2:3] - 0.6
    level = (iota((1, K), 1) & 3).astype(F32)
    hs = []
    ds = []
    for m in range(MB):
        brick = jnp.maximum(occ[0, m], 0)
        hs.append(3.0 * lines[0, pl.ds(brick, 1), :] - 1.5)
        ds.append(lines[1, pl.ds(brick, 1), :] - 0.5)
    hd = jnp.concatenate(hs + ds + [jnp.zeros((112, 128), F32)], axis=0)
    hdt = hd.T
    for d in range(NV):
        for m in range(MB):
            h = hdt[d * SHARE:(d + 1) * SHARE, m:m + 1]
            e = hdt[d * SHARE:(d + 1) * SHARE, MB + m:MB + m + 1]
            pos = centre + tilt * h + sweep * e
            w = jnp.maximum(0.0, 1.0 - jnp.abs(pos - level))
            wgt[pl.ds(d * CHUNK + m * SHARE, SHARE), :] = w.astype(BF16)

    drain(mrcv.at[pl.ds(0, NS - 1)], mr)
    mrcv[pl.ds(s, 1)] = msnd[...]
    here = (iota((128, 128), 0) == s).astype(F32).astype(BF16)
    marks = jnp.dot(mrcv[...].reshape(2 * NS, 128), here, preferred_element_type=F32).astype(BF16)
    twice = ((iota((K, 2 * NS), 0) >> 1) == iota((K, 2 * NS), 1)).astype(F32).astype(BF16)
    marks = jnp.dot(twice, marks, preferred_element_type=F32).astype(BF16)

    drain(rcv.at[pl.ds(0, NS - 1)], rs)
    rcv[pl.ds(s, 1)] = snd[pl.ds(s, 1)]
    both = jnp.concatenate([rcv[...].reshape(K, 128), marks], axis=1)
    diag = iota((128, 128), 0) == iota((128, 128), 1)

    def chunk(d):
        r = jnp.dot(wgt[pl.ds(pl.multiple_of(d * CHUNK, CHUNK), CHUNK), :], both, preferred_element_type=F32)
        ray = jnp.sum(jnp.where(diag, r[:, 128:], 0.0), axis=0, keepdims=True)
        return r[:, :128], ray

    rowid = iota((16, 128), 0)
    for d in (4, 3, 5, 2, 6, 1, 7):
        t = (y + d) & 7
        num, ray = chunk(t)
        hi = ray.astype(BF16)
        lo = (ray - hi.astype(F32)).astype(BF16)
        part[t, 0:CHUNK, :] = num.astype(BF16)
        hilo = jnp.where(rowid == 0, hi.astype(F32), jnp.where(rowid == 1, lo.astype(F32), 0.0))
        part[t, CHUNK:MSG, :] = hilo.astype(BF16)
        pltpu.make_async_remote_copy(
            src_ref=part.at[t], dst_ref=got.at[y], send_sem=ss2, recv_sem=rs2,
            device_id=(s, t), device_id_type=MESH,
        ).start()
    num, ray = chunk(y)
    got[pl.ds(y, 1)] = jnp.zeros((1, MSG, 128), BF16)
    fetch[6].wait()
    drain(snd.at[pl.ds(0, NS - 1)], ss)
    drain(mrcv.at[pl.ds(0, NS - 1)], ms)
    drain(got.at[pl.ds(0, NV - 1)], rs2)
    for v in range(NV):
        num = num + got[v, 0:CHUNK, :].astype(F32)
        tail = got[v, CHUNK:MSG, :].astype(F32)
        ray = ray + (tail[0:1] + tail[1:2])
    rayc = jnp.broadcast_to(ray, (128, 128)).T
    new = RELAX * num / (rayc + SHIFT)
    upd[0:MB] = new.reshape(MB, SHARE, 128)
    upd[MB:MB + 1] = jnp.zeros((1, SHARE, 128), F32)
    for b in range(16):
        slot = jnp.int32(MB)
        for m in range(MB):
            slot = jnp.where(occ[0, m] == b, m, slot)
        out[b] = vol[b] + upd[slot]
    drain(part.at[pl.ds(0, NV - 1)], ss2)


def per_device(residual, route_list, tile_offsets, view_geometry, line_coords, occupied, volume):
    hbm = pl.BlockSpec(memory_space=pltpu.HBM)
    sem = pltpu.SemaphoreType.DMA
    return pl.pallas_call(
        body,
        out_shape=jax.ShapeDtypeStruct(volume.shape, F32),
        in_specs=[hbm] * 7,
        out_specs=pl.BlockSpec(memory_space=pltpu.VMEM),
        scratch_shapes=[
            pltpu.SMEM((VIEWS,), jnp.int32),
            pltpu.SMEM((1, MB), jnp.int32),
            pltpu.VMEM((384, 128), BF16),
            pltpu.VMEM((1, 2, NS), jnp.int32),
            pltpu.VMEM((4, VIEWS), F32),
            pltpu.VMEM((2, 16, 128), F32),
            pltpu.VMEM((16, SHARE, 128), F32),
            pltpu.VMEM((NS, ROWS, 128), BF16),
            pltpu.VMEM((NS, ROWS, 128), BF16),
            pltpu.VMEM((1, 2, 128), BF16),
            pltpu.VMEM((NS, 2, 128), BF16),
            pltpu.VMEM((NV * CHUNK, K), BF16),
            pltpu.VMEM((NV, MSG, 128), BF16),
            pltpu.VMEM((NV, MSG, 128), BF16),
            pltpu.VMEM((MB + 1, SHARE, 128), F32),
            sem((7,)), sem, sem, sem, sem, sem, sem,
        ],
        compiler_params=pltpu.CompilerParams(
            collective_id=0, has_side_effects=True, vmem_limit_bytes=60 << 20
        ),
    )(
        tile_offsets, occupied, residual.reshape(384, 128), jnp.swapaxes(route_list, 1, 2),
        view_geometry, line_coords, volume,
    )


def solution(mesh):
    placed = (
        P(("view", "slab"), None, None, None),
        P(("view", "slab"), None, None),
        P(),
        P(),
        P(None, "slab", None),
        P("slab", None),
        P("slab", "view", None),
    )
    return jax.shard_map(
        per_device, mesh=mesh, in_specs=placed, out_specs=P("slab", "view", None), check_vma=False
    )
```

```python
import jax
import jax.numpy as jnp
from jax import lax
from jax.experimental import pallas as pl
from jax.experimental.pallas import tpu as pltpu
from jax.sharding import PartitionSpec as P

MESH = pl.DeviceIdType.MESH
F32 = jnp.float32
BF16 = jnp.bfloat16

NS = 96
NV = 8
VIEWS = 768
ROWS = 4
K = NS * ROWS
MB = 8
SHARE = 16
CHUNK = MB * SHARE
RELAX = 0.9
SHIFT = 0.1 * VIEWS


def iota(shape, dim):
    return lax.broadcasted_iota(jnp.int32, shape, dim)


def drain(ref, sem):
    pltpu.make_async_copy(ref, ref, sem).wait()


def ring(v, step, n):
    t = v + step
    return jnp.where(t >= n, t - n, t)


def peers(s, act):
    x = s // 24
    z = (s - 24 * x) >> 1
    c = s & 1
    bases = [24 * ((x + dx) & 3) + (c ^ dc) for dx in (2, 1, 3, 0) for dc in (1, 0)]

    def column(i, carry):
        dz = jnp.where(i >= 6, i - 5, i + 6)
        t = 2 * ring(z, dz, 12)
        for base in bases:
            act(base + t)
        return carry

    lax.fori_loop(0, 11, column, 0)
    for base in bases[:-1]:
        act(base + 2 * z)


def body(
    offs_h, occ_h, res_h, route_h, geo_h, lines_h, vol_h, out,
    offs, occ, res, route, geo, lines, vol,
    snd, rcv, mrcv, wgt, part, got, rpart, rgot, upd, ins, ss, rs, ms, mr, ms2, mr2, ss2, rs2, ss3, rs3,
):
    s = lax.axis_index("slab")
    y = lax.axis_index("view")
    view = y * NS + s
    x = s // 24
    z = (s - 24 * x) >> 1
    core = s & 1
    k = 2 * x + core

    fetch = [
        pltpu.make_async_copy(h, v, ins.at[i])
        for i, (h, v) in enumerate(
            [
                (res_h, res), (route_h, route), (geo_h, geo), (offs_h, offs),
                (occ_h, occ), (lines_h, lines), (vol_h, vol),
            ]
        )
    ]
    for f in fetch:
        f.start()

    bar = pltpu.get_barrier_semaphore()

    def greet(p):
        pl.semaphore_signal(bar, inc=1, device_id=(p, y), device_id_type=MESH)

    peers(s, greet)
    for d in range(1, NV):
        pl.semaphore_signal(bar, inc=1, device_id=(s, (y + d) & 7), device_id_type=MESH)

    for f in fetch[:4]:
        f.wait()
    g = geo[...]
    lane = iota((4, VIEWS), 1)
    mine = jnp.sum(jnp.where(lane == view, g, 0.0), axis=1, keepdims=True)
    slope = 0.8 + 0.05 * mine[3:4, :]
    off = offs[view].astype(F32)
    col = iota((128, 128), 0).astype(F32)
    xs = iota((128, 128), 1).astype(F32)
    table = jnp.maximum(0.0, 1.0 - jnp.abs(col - (off + slope * xs))).astype(BF16)
    proj = jnp.dot(res[...], table, preferred_element_type=F32).astype(BF16)

    blocks = route[0].astype(F32)
    listed = blocks.astype(BF16)
    owner = (iota((K, NS), 0) >> 2) == iota((K, NS), 1)
    spread = lax.dot_general(
        owner.astype(F32).astype(BF16), listed, (((1,), (1,)), ((), ())), preferred_element_type=F32
    )
    q = iota((K, 1), 0) & 3
    block = jnp.where(q < 2, spread[:, 0:1], spread[:, 1:2])
    want = 2.0 * block + (q & 1).astype(F32)
    pick = (iota((K, 384), 1).astype(F32) == want).astype(F32).astype(BF16)
    tile = jnp.dot(pick, proj, preferred_element_type=F32)
    snd[...] = tile.astype(BF16).reshape(NS, ROWS, 128)
    flags = jnp.where(blocks >= 0.0, 1.0, 0.0)
    flags = jnp.concatenate([flags, jnp.zeros((2, 128 - NS), F32)], axis=1)
    mrcv[pl.ds(k, 1), pl.ds(z, 1)] = flags.astype(BF16).reshape(1, 1, 2, 128)

    pl.semaphore_wait(bar, NS - 1 + NV - 1)

    def send_marks(i, c):
        dz = jnp.where(i >= 6, i - 5, i + 6)
        t = ring(z, dz, 12)
        pltpu.make_async_remote_copy(
            src_ref=mrcv.at[k, z], dst_ref=mrcv.at[k, z], send_sem=ms, recv_sem=mr,
            device_id=(24 * x + 2 * t + core, y), device_id_type=MESH,
        ).start()
        return c

    lax.fori_loop(0, 11, send_marks, 0)

    def send(p):
        pltpu.make_async_remote_copy(
            src_ref=snd.at[p], dst_ref=rcv.at[s], send_sem=ss, recv_sem=rs,
            device_id=(p, y), device_id_type=MESH,
        ).start()

    peers(s, send)

    for f in fetch[4:6]:
        f.wait()
    g1 = g.astype(BF16)
    r1 = g - g1.astype(F32)
    g2 = r1.astype(BF16)
    g3 = (r1 - g2.astype(F32)).astype(BF16)
    sel = (iota((VIEWS, K), 0) - y * NS) == (iota((VIEWS, K), 1) >> 2)
    sel = sel.astype(F32).astype(BF16)
    gg = (
        jnp.dot(g1, sel, preferred_element_type=F32)
        + jnp.dot(g2, sel, preferred_element_type=F32)
        + jnp.dot(g3, sel, preferred_element_type=F32)
    )
    centre = 1.25 + 0.5 * gg[0:1]
    tilt = 0.6 + 0.6 * gg[1:2]
    sweep = 1.2 * gg[2:3] - 0.6
    level = (iota((1, K), 1) & 3).astype(F32)
    def forward_marks():
        drain(mrcv.at[0, pl.ds(0, 11)], mr)
        for dx, dc in ((2, 1), (2, 0), (1, 1), (3, 1), (1, 0), (3, 0), (0, 1)):
            p = 24 * ((x + dx) & 3) + 2 * z + (core ^ dc)
            pltpu.make_async_remote_copy(
                src_ref=mrcv.at[k], dst_ref=mrcv.at[k], send_sem=ms2, recv_sem=mr2,
                device_id=(p, y), device_id_type=MESH,
            ).start()

    hs = []
    ds = []
    for m in range(MB):
        brick = jnp.maximum(occ[0, m], 0)
        hs.append(3.0 * lines[0, pl.ds(brick, 1), :] - 1.5)
        ds.append(lines[1, pl.ds(brick, 1), :] - 0.5)
    hd = jnp.concatenate(hs + ds + [jnp.zeros((112, 128), F32)], axis=0)
    hdt = hd.T
    for d in range(NV):
        for m in range(MB):
            h = hdt[d * SHARE:(d + 1) * SHARE, m:m + 1]
            e = hdt[d * SHARE:(d + 1) * SHARE, MB + m:MB + m + 1]
            pos = centre + tilt * h + sweep * e
            w = jnp.maximum(0.0, 1.0 - jnp.abs(pos - level))
            wgt[pl.ds(d * CHUNK + m * SHARE, SHARE), :] = w.astype(BF16)
    forward_marks()

    drain(mrcv.at[pl.ds(0, 7)], mr2)
    here = (iota((128, 128), 0) == s).astype(F32).astype(BF16)
    marks = jnp.dot(mrcv[...].reshape(2 * NS, 128), here, preferred_element_type=F32).astype(BF16)
    r = iota((K, 1), 0)
    a = r >> 2
    xa = (a >= 24).astype(jnp.int32) + (a >= 48).astype(jnp.int32) + (a >= 72).astype(jnp.int32)
    place = 24 * (2 * xa + (a & 1)) + 2 * ((a - 24 * xa) >> 1) + ((r >> 1) & 1)
    twice = (place == iota((K, 2 * NS), 1)).astype(F32).astype(BF16)
    marks = jnp.dot(twice, marks, preferred_element_type=F32).astype(BF16)

    drain(rcv.at[pl.ds(0, NS - 1)], rs)
    rcv[pl.ds(s, 1)] = snd[pl.ds(s, 1)]
    both = jnp.concatenate([rcv[...].reshape(K, 128), marks], axis=1)
    diag = iota((128, 128), 0) == iota((128, 128), 1)

    def chunk(d):
        r = jnp.dot(wgt[pl.ds(pl.multiple_of(d * CHUNK, CHUNK), CHUNK), :], both, preferred_element_type=F32)
        ray = jnp.sum(jnp.where(diag, r[:, 128:], 0.0), axis=0, keepdims=True)
        return r[:, :128], ray

    for d in (4, 3, 5, 2, 6, 1, 7):
        t = (y + d) & 7
        num, ray = chunk(t)
        hi = ray.astype(BF16)
        lo = (ray - hi.astype(F32)).astype(BF16)
        part[t] = num.astype(BF16)
        hilo = jnp.concatenate([hi.astype(F32), lo.astype(F32)], axis=0)
        rpart[pl.ds(t, 1)] = hilo.astype(BF16).reshape(1, 2, 128)
        pltpu.make_async_remote_copy(
            src_ref=part.at[t], dst_ref=got.at[y], send_sem=ss2, recv_sem=rs2,
            device_id=(s, t), device_id_type=MESH,
        ).start()
        pltpu.make_async_remote_copy(
            src_ref=rpart.at[t], dst_ref=rgot.at[y], send_sem=ss3, recv_sem=rs3,
            device_id=(s, t), device_id_type=MESH,
        ).start()
    num, ray = chunk(y)
    got[pl.ds(y, 1)] = jnp.zeros((1, CHUNK, 128), BF16)
    rgot[pl.ds(y, 1)] = jnp.zeros((1, 2, 128), BF16)
    fetch[6].wait()
    drain(snd.at[pl.ds(0, NS - 1)], ss)
    drain(mrcv.at[0, pl.ds(0, 11)], ms)
    drain(mrcv.at[pl.ds(0, 7)], ms2)
    drain(rgot.at[pl.ds(0, NV - 1)], rs3)
    drain(got.at[pl.ds(0, NV - 1)], rs2)
    for v in range(NV):
        num = num + got[v].astype(F32)
        tail = rgot[v].astype(F32)
        ray = ray + (tail[0:1] + tail[1:2])
    rayc = jnp.broadcast_to(ray, (128, 128)).T
    new = RELAX * num / (rayc + SHIFT)
    upd[0:MB] = new.reshape(MB, SHARE, 128)
    upd[MB:MB + 1] = jnp.zeros((1, SHARE, 128), F32)
    for b in range(16):
        slot = jnp.int32(MB)
        for m in range(MB):
            slot = jnp.where(occ[0, m] == b, m, slot)
        out[b] = vol[b] + upd[slot]
    drain(part.at[pl.ds(0, NV - 1)], ss2)
    drain(rpart.at[pl.ds(0, NV - 1)], ss3)


def per_device(residual, route_list, tile_offsets, view_geometry, line_coords, occupied, volume):
    hbm = pl.BlockSpec(memory_space=pltpu.HBM)
    sem = pltpu.SemaphoreType.DMA
    return pl.pallas_call(
        body,
        out_shape=jax.ShapeDtypeStruct(volume.shape, F32),
        in_specs=[hbm] * 7,
        out_specs=pl.BlockSpec(memory_space=pltpu.VMEM),
        scratch_shapes=[
            pltpu.SMEM((VIEWS,), jnp.int32),
            pltpu.SMEM((1, MB), jnp.int32),
            pltpu.VMEM((384, 128), BF16),
            pltpu.VMEM((1, 2, NS), jnp.int32),
            pltpu.VMEM((4, VIEWS), F32),
            pltpu.VMEM((2, 16, 128), F32),
            pltpu.VMEM((16, SHARE, 128), F32),
            pltpu.VMEM((NS, ROWS, 128), BF16),
            pltpu.VMEM((NS, ROWS, 128), BF16),
            pltpu.VMEM((8, 12, 2, 128), BF16),
            pltpu.VMEM((NV * CHUNK, K), BF16),
            pltpu.VMEM((NV, CHUNK, 128), BF16),
            pltpu.VMEM((NV, CHUNK, 128), BF16),
            pltpu.VMEM((NV, 2, 128), BF16),
            pltpu.VMEM((NV, 2, 128), BF16),
            pltpu.VMEM((MB + 1, SHARE, 128), F32),
            sem((7,)), sem, sem, sem, sem, sem, sem, sem, sem, sem, sem,
        ],
        compiler_params=pltpu.CompilerParams(
            collective_id=0, has_side_effects=True, vmem_limit_bytes=60 << 20
        ),
    )(
        tile_offsets, occupied, residual.reshape(384, 128), jnp.swapaxes(route_list, 1, 2),
        view_geometry, line_coords, volume,
    )


def solution(mesh):
    placed = (
        P(("view", "slab"), None, None, None),
        P(("view", "slab"), None, None),
        P(),
        P(),
        P(None, "slab", None),
        P("slab", None),
        P("slab", "view", None),
    )
    return jax.shard_map(
        per_device, mesh=mesh, in_specs=placed, out_specs=P("slab", "view", None), check_vma=False
    )
```

```python
import jax
import jax.numpy as jnp
from jax import lax
from jax.experimental import pallas as pl
from jax.experimental.pallas import tpu as pltpu
from jax.sharding import PartitionSpec as P

MESH = pl.DeviceIdType.MESH
F32 = jnp.float32
BF16 = jnp.bfloat16

NS = 96
NV = 8
VIEWS = 768
ROWS = 4
K = NS * ROWS
MB = 8
SHARE = 16
CHUNK = MB * SHARE
RELAX = 0.9
SHIFT = 0.1 * VIEWS


def iota(shape, dim):
    return lax.broadcasted_iota(jnp.int32, shape, dim)


def drain(ref, sem):
    pltpu.make_async_copy(ref, ref, sem).wait()


def ring(v, step, n):
    t = v + step
    return jnp.where(t >= n, t - n, t)


def peers(s, act):
    x = s // 24
    z = (s - 24 * x) >> 1
    c = s & 1
    bases = [24 * ((x + dx) & 3) + (c ^ dc) for dx in (2, 1, 3, 0) for dc in (1, 0)]

    def column(i, carry):
        dz = jnp.where(i >= 6, i - 5, i + 6)
        t = 2 * ring(z, dz, 12)
        for base in bases:
            act(base + t)
        return carry

    lax.fori_loop(0, 11, column, 0)
    for base in bases[:-1]:
        act(base + 2 * z)


def body(
    offs_h, occ_h, res_h, route_h, geo_h, lines_h, vol_h, out,
    offs, occ, res, route, geo, lines, vol,
    snd, rcv, mrcv, wgt, part, got, rpart, rgot, upd, ins, ss, rs, ms, mr, ms2, mr2, ss2, rs2, ss3, rs3,
):
    s = lax.axis_index("slab")
    y = lax.axis_index("view")
    view = y * NS + s
    x = s // 24
    z = (s - 24 * x) >> 1
    core = s & 1
    k = 2 * x + core

    fetch = [
        pltpu.make_async_copy(h, v, ins.at[i])
        for i, (h, v) in enumerate(
            [
                (res_h, res), (route_h, route), (geo_h, geo), (offs_h, offs),
                (occ_h, occ), (lines_h, lines), (vol_h, vol),
            ]
        )
    ]
    for i in (1, 0, 2, 3, 4, 5, 6):
        fetch[i].start()

    bar = pltpu.get_barrier_semaphore()

    def greet(p):
        pl.semaphore_signal(bar, inc=1, device_id=(p, y), device_id_type=MESH)

    peers(s, greet)
    for d in range(1, NV):
        pl.semaphore_signal(bar, inc=1, device_id=(s, (y + d) & 7), device_id_type=MESH)

    fetch[1].wait()
    blocks = route[0].astype(F32)
    listed = blocks.astype(BF16)
    owner = (iota((K, NS), 0) >> 2) == iota((K, NS), 1)
    spread = lax.dot_general(
        owner.astype(F32).astype(BF16), listed, (((1,), (1,)), ((), ())), preferred_element_type=F32
    )
    q = iota((K, 1), 0) & 3
    block = jnp.where(q < 2, spread[:, 0:1], spread[:, 1:2])
    want = 2.0 * block + (q & 1).astype(F32)
    pick = (iota((K, 384), 1).astype(F32) == want).astype(F32).astype(BF16)
    flags = jnp.where(blocks >= 0.0, 1.0, 0.0)
    flags = jnp.concatenate([flags, jnp.zeros((2, 128 - NS), F32)], axis=1)
    mrcv[pl.ds(k, 1), pl.ds(z, 1)] = flags.astype(BF16).reshape(1, 1, 2, 128)

    fetch[2].wait()
    fetch[3].wait()
    g = geo[...]
    lane = iota((4, VIEWS), 1)
    mine = jnp.sum(jnp.where(lane == view, g, 0.0), axis=1, keepdims=True)
    slope = 0.8 + 0.05 * mine[3:4, :]
    off = offs[view].astype(F32)
    col = iota((128, 128), 0).astype(F32)
    xs = iota((128, 128), 1).astype(F32)
    table = jnp.maximum(0.0, 1.0 - jnp.abs(col - (off + slope * xs))).astype(BF16)
    fetch[0].wait()
    proj = jnp.dot(res[...], table, preferred_element_type=F32).astype(BF16)
    tile = jnp.dot(pick, proj, preferred_element_type=F32)
    snd[...] = tile.astype(BF16).reshape(NS, ROWS, 128)

    pl.semaphore_wait(bar, NS - 1 + NV - 1)

    def send_marks(i, c):
        dz = jnp.where(i >= 6, i - 5, i + 6)
        t = ring(z, dz, 12)
        pltpu.make_async_remote_copy(
            src_ref=mrcv.at[k, z], dst_ref=mrcv.at[k, z], send_sem=ms, recv_sem=mr,
            device_id=(24 * x + 2 * t + core, y), device_id_type=MESH,
        ).start()
        return c

    lax.fori_loop(0, 11, send_marks, 0)

    def send(p):
        pltpu.make_async_remote_copy(
            src_ref=snd.at[p], dst_ref=rcv.at[s], send_sem=ss, recv_sem=rs,
            device_id=(p, y), device_id_type=MESH,
        ).start()

    peers(s, send)

    for f in fetch[4:6]:
        f.wait()
    g1 = g.astype(BF16)
    r1 = g - g1.astype(F32)
    g2 = r1.astype(BF16)
    g3 = (r1 - g2.astype(F32)).astype(BF16)
    sel = (iota((VIEWS, K), 0) - y * NS) == (iota((VIEWS, K), 1) >> 2)
    sel = sel.astype(F32).astype(BF16)
    gg = (
        jnp.dot(g1, sel, preferred_element_type=F32)
        + jnp.dot(g2, sel, preferred_element_type=F32)
        + jnp.dot(g3, sel, preferred_element_type=F32)
    )
    centre = 1.25 + 0.5 * gg[0:1]
    tilt = 0.6 + 0.6 * gg[1:2]
    sweep = 1.2 * gg[2:3] - 0.6
    level = (iota((1, K), 1) & 3).astype(F32)
    def forward_marks():
        drain(mrcv.at[0, pl.ds(0, 11)], mr)
        for dx, dc in ((2, 1), (2, 0), (1, 1), (3, 1), (1, 0), (3, 0), (0, 1)):
            p = 24 * ((x + dx) & 3) + 2 * z + (core ^ dc)
            pltpu.make_async_remote_copy(
                src_ref=mrcv.at[k], dst_ref=mrcv.at[k], send_sem=ms2, recv_sem=mr2,
                device_id=(p, y), device_id_type=MESH,
            ).start()

    hs = []
    ds = []
    for m in range(MB):
        brick = jnp.maximum(occ[0, m], 0)
        hs.append(3.0 * lines[0, pl.ds(brick, 1), :] - 1.5)
        ds.append(lines[1, pl.ds(brick, 1), :] - 0.5)
    hd = jnp.concatenate(hs + ds + [jnp.zeros((112, 128), F32)], axis=0)
    hdt = hd.T
    for d in range(NV):
        for m in range(MB):
            h = hdt[d * SHARE:(d + 1) * SHARE, m:m + 1]
            e = hdt[d * SHARE:(d + 1) * SHARE, MB + m:MB + m + 1]
            pos = centre + tilt * h + sweep * e
            w = jnp.maximum(0.0, 1.0 - jnp.abs(pos - level))
            wgt[pl.ds(d * CHUNK + m * SHARE, SHARE), :] = w.astype(BF16)
    forward_marks()

    slots = []
    for b in range(16):
        slot = jnp.int32(MB)
        for m in range(MB):
            slot = jnp.where(occ[0, m] == b, m, slot)
        slots.append(slot)
    r = iota((K, 1), 0)
    a = r >> 2
    xa = (a >= 24).astype(jnp.int32) + (a >= 48).astype(jnp.int32) + (a >= 72).astype(jnp.int32)
    place = 24 * (2 * xa + (a & 1)) + 2 * ((a - 24 * xa) >> 1) + ((r >> 1) & 1)
    twice = (place == iota((K, 2 * NS), 1)).astype(F32).astype(BF16)
    here = (iota((128, 128), 0) == s).astype(F32).astype(BF16)
    diag = iota((128, 128), 0) == iota((128, 128), 1)
    fetch[6].wait()

    drain(rcv.at[pl.ds(0, NS - 1)], rs)
    rcv[pl.ds(s, 1)] = snd[pl.ds(s, 1)]
    rows = rcv[...].reshape(K, 128)

    def chunk(d, right):
        left = wgt[pl.ds(pl.multiple_of(d * CHUNK, CHUNK), CHUNK), :]
        return jnp.dot(left, right, preferred_element_type=F32)

    for d in (4, 3, 5, 2, 6, 1, 7):
        t = (y + d) & 7
        part[t] = chunk(t, rows).astype(BF16)
        pltpu.make_async_remote_copy(
            src_ref=part.at[t], dst_ref=got.at[y], send_sem=ss2, recv_sem=rs2.at[y],
            device_id=(s, t), device_id_type=MESH,
        ).start()

    drain(mrcv.at[pl.ds(0, 7)], mr2)
    marks = jnp.dot(mrcv[...].reshape(2 * NS, 128), here, preferred_element_type=F32).astype(BF16)
    marks = jnp.dot(twice, marks, preferred_element_type=F32).astype(BF16)

    def ray_of(d):
        return jnp.sum(jnp.where(diag, chunk(d, marks), 0.0), axis=0, keepdims=True)

    for d in (4, 3, 5, 2, 6, 1, 7):
        t = (y + d) & 7
        ray = ray_of(t)
        hi = ray.astype(BF16)
        lo = (ray - hi.astype(F32)).astype(BF16)
        hilo = jnp.concatenate([hi.astype(F32), lo.astype(F32)], axis=0)
        rpart[pl.ds(t, 1)] = hilo.astype(BF16).reshape(1, 2, 128)
        pltpu.make_async_remote_copy(
            src_ref=rpart.at[t], dst_ref=rgot.at[y], send_sem=ss3, recv_sem=rs3,
            device_id=(s, t), device_id_type=MESH,
        ).start()

    num = chunk(y, rows)
    ray = ray_of(y)
    upd[MB:MB + 1] = jnp.zeros((1, SHARE, 128), F32)
    rgot[pl.ds(y, 1)] = jnp.zeros((1, 2, 128), BF16)
    drain(snd.at[pl.ds(0, NS - 1)], ss)
    drain(mrcv.at[0, pl.ds(0, 11)], ms)
    drain(mrcv.at[pl.ds(0, 7)], ms2)
    for d in (1, 7, 2, 6, 3, 5, 4):
        v = (y + d) & 7
        drain(got.at[v], rs2.at[v])
        num = num + got[v].astype(F32)
    drain(rgot.at[pl.ds(0, NV - 1)], rs3)
    for v in range(NV):
        tail = rgot[v].astype(F32)
        ray = ray + (tail[0:1] + tail[1:2])
    rayc = jnp.broadcast_to(ray, (128, 128)).T
    new = RELAX * num / (rayc + SHIFT)
    upd[0:MB] = new.reshape(MB, SHARE, 128)
    for b in range(16):
        out[b] = vol[b] + upd[slots[b]]
    drain(part.at[pl.ds(0, NV - 1)], ss2)
    drain(rpart.at[pl.ds(0, NV - 1)], ss3)


def per_device(residual, route_list, tile_offsets, view_geometry, line_coords, occupied, volume):
    hbm = pl.BlockSpec(memory_space=pltpu.HBM)
    sem = pltpu.SemaphoreType.DMA
    return pl.pallas_call(
        body,
        out_shape=jax.ShapeDtypeStruct(volume.shape, F32),
        in_specs=[hbm] * 7,
        out_specs=pl.BlockSpec(memory_space=pltpu.VMEM),
        scratch_shapes=[
            pltpu.SMEM((VIEWS,), jnp.int32),
            pltpu.SMEM((1, MB), jnp.int32),
            pltpu.VMEM((384, 128), BF16),
            pltpu.VMEM((1, 2, NS), jnp.int32),
            pltpu.VMEM((4, VIEWS), F32),
            pltpu.VMEM((2, 16, 128), F32),
            pltpu.VMEM((16, SHARE, 128), F32),
            pltpu.VMEM((NS, ROWS, 128), BF16),
            pltpu.VMEM((NS, ROWS, 128), BF16),
            pltpu.VMEM((8, 12, 2, 128), BF16),
            pltpu.VMEM((NV * CHUNK, K), BF16),
            pltpu.VMEM((NV, CHUNK, 128), BF16),
            pltpu.VMEM((NV, CHUNK, 128), BF16),
            pltpu.VMEM((NV, 2, 128), BF16),
            pltpu.VMEM((NV, 2, 128), BF16),
            pltpu.VMEM((MB + 1, SHARE, 128), F32),
            sem((7,)), sem, sem, sem, sem, sem, sem, sem, sem((NV,)), sem, sem,
        ],
        compiler_params=pltpu.CompilerParams(
            collective_id=0, has_side_effects=True, vmem_limit_bytes=60 << 20
        ),
    )(
        tile_offsets, occupied, residual.reshape(384, 128), jnp.swapaxes(route_list, 1, 2),
        view_geometry, line_coords, volume,
    )


def solution(mesh):
    placed = (
        P(("view", "slab"), None, None, None),
        P(("view", "slab"), None, None),
        P(),
        P(),
        P(None, "slab", None),
        P("slab", None),
        P("slab", "view", None),
    )
    return jax.shard_map(
        per_device, mesh=mesh, in_specs=placed, out_specs=P("slab", "view", None), check_vma=False
    )
```

```python
import jax
import jax.numpy as jnp
from jax import lax
from jax.experimental import pallas as pl
from jax.experimental.pallas import tpu as pltpu
from jax.sharding import PartitionSpec as P

MESH = pl.DeviceIdType.MESH
F32 = jnp.float32
BF16 = jnp.bfloat16

NS = 96
NV = 8
VIEWS = 768
ROWS = 4
K = NS * ROWS
MB = 8
SHARE = 16
CHUNK = MB * SHARE
RELAX = 0.9
SHIFT = 0.1 * VIEWS


def iota(shape, dim):
    return lax.broadcasted_iota(jnp.int32, shape, dim)


def drain(ref, sem):
    pltpu.make_async_copy(ref, ref, sem).wait()


def ring(v, step, n):
    t = v + step
    return jnp.where(t >= n, t - n, t)


def peers(s, act, twin=None):
    x = s // 24
    z = (s - 24 * x) >> 1
    c = s & 1
    bases = [(dc, 24 * ((x + dx) & 3) + (c ^ dc)) for dx in (2, 1, 3, 0) for dc in (0, 1)]

    def visit(dc, p):
        if twin is not None and dc == 0:
            twin(p)
        act(p)

    def column(i, carry):
        dz = 6 + ((i + 1) >> 1) * (1 - 2 * (i & 1))
        t = 2 * ring(z, dz, 12)
        for dc, base in bases:
            visit(dc, base + t)
        return carry

    lax.fori_loop(0, 11, column, 0)
    for dc, base in bases[:6] + bases[7:]:
        visit(dc, base + 2 * z)


def body(
    offs_h, occ_h, res_h, route_h, geo_h, lines_h, vol_h, out,
    offs, occ, res, route, geo, lines, vol,
    snd, rcv, mrcv, wgt, part, got, rpart, rgot, upd, ins, ss, rs, ms, mr, ms2, mr2, ss2, rs2, ss3, rs3,
):
    s = lax.axis_index("slab")
    y = lax.axis_index("view")
    view = y * NS + s
    x = s // 24
    z = (s - 24 * x) >> 1
    core = s & 1
    chip = s >> 1

    fetch = [
        pltpu.make_async_copy(h, v, ins.at[i])
        for i, (h, v) in enumerate(
            [
                (res_h, res), (route_h, route), (geo_h, geo), (offs_h, offs),
                (occ_h, occ), (lines_h, lines), (vol_h, vol),
            ]
        )
    ]
    for f in fetch:
        f.start()

    bar = pltpu.get_barrier_semaphore()

    def greet(p):
        pl.semaphore_signal(bar, inc=1, device_id=(p, y), device_id_type=MESH)

    peers(s, greet)
    for d in range(1, NV):
        pl.semaphore_signal(bar, inc=1, device_id=(s, (y + d) & 7), device_id_type=MESH)

    for f in fetch[:4]:
        f.wait()
    g = geo[...]
    lane = iota((4, VIEWS), 1)
    mine = jnp.sum(jnp.where(lane == view, g, 0.0), axis=1, keepdims=True)
    slope = 0.8 + 0.05 * mine[3:4, :]
    off = offs[view].astype(F32)
    col = iota((128, 128), 0).astype(F32)
    xs = iota((128, 128), 1).astype(F32)
    table = jnp.maximum(0.0, 1.0 - jnp.abs(col - (off + slope * xs))).astype(BF16)
    proj = jnp.dot(res[...], table, preferred_element_type=F32).astype(BF16)

    blocks = route[0].astype(F32)
    listed = blocks.astype(BF16)
    owner = (iota((K, NS), 0) >> 2) == iota((K, NS), 1)
    spread = lax.dot_general(
        owner.astype(F32).astype(BF16), listed, (((1,), (1,)), ((), ())), preferred_element_type=F32
    )
    q = iota((K, 1), 0) & 3
    block = jnp.where(q < 2, spread[:, 0:1], spread[:, 1:2])
    want = 2.0 * block + (q & 1).astype(F32)
    pick = (iota((K, 384), 1).astype(F32) == want).astype(F32).astype(BF16)
    tile = jnp.dot(pick, proj, preferred_element_type=F32)
    snd[...] = tile.astype(BF16).reshape(NS, ROWS, 128)
    flags = jnp.where(blocks >= 0.0, 1.0, 0.0)
    flags = jnp.concatenate([flags, jnp.zeros((2, 128 - NS), F32)], axis=1)
    mrcv[pl.ds(core, 1), pl.ds(chip, 1)] = flags.astype(BF16).reshape(1, 1, 2, 128)

    pl.semaphore_wait(bar, NS - 1 + NV - 1)

    def send(p):
        pltpu.make_async_remote_copy(
            src_ref=snd.at[p], dst_ref=rcv.at[s], send_sem=ss, recv_sem=rs,
            device_id=(p, y), device_id_type=MESH,
        ).start()

    def send_marks(p):
        pltpu.make_async_remote_copy(
            src_ref=mrcv.at[core, chip], dst_ref=mrcv.at[core, chip], send_sem=ms, recv_sem=mr,
            device_id=(p, y), device_id_type=MESH,
        ).start()

    peers(s, send, send_marks)

    for f in fetch[4:6]:
        f.wait()
    g1 = g.astype(BF16)
    r1 = g - g1.astype(F32)
    g2 = r1.astype(BF16)
    g3 = (r1 - g2.astype(F32)).astype(BF16)
    sel = (iota((VIEWS, K), 0) - y * NS) == (iota((VIEWS, K), 1) >> 2)
    sel = sel.astype(F32).astype(BF16)
    gg = (
        jnp.dot(g1, sel, preferred_element_type=F32)
        + jnp.dot(g2, sel, preferred_element_type=F32)
        + jnp.dot(g3, sel, preferred_element_type=F32)
    )
    centre = 1.25 + 0.5 * gg[0:1]
    tilt = 0.6 + 0.6 * gg[1:2]
    sweep = 1.2 * gg[2:3] - 0.6
    level = (iota((1, K), 1) & 3).astype(F32)
    def forward_marks():
        drain(mrcv.at[0, pl.ds(0, 47)], mr)
        pltpu.make_async_remote_copy(
            src_ref=mrcv.at[core], dst_ref=mrcv.at[core], send_sem=ms2, recv_sem=mr2,
            device_id=(s ^ 1, y), device_id_type=MESH,
        ).start()

    hs = []
    ds = []
    for m in range(MB):
        brick = jnp.maximum(occ[0, m], 0)
        hs.append(3.0 * lines[0, pl.ds(brick, 1), :] - 1.5)
        ds.append(lines[1, pl.ds(brick, 1), :] - 0.5)
    hd = jnp.concatenate(hs + ds + [jnp.zeros((112, 128), F32)], axis=0)
    hdt = hd.T
    for d in range(NV):
        for m in range(MB):
            h = hdt[d * SHARE:(d + 1) * SHARE, m:m + 1]
            e = hdt[d * SHARE:(d + 1) * SHARE, MB + m:MB + m + 1]
            pos = centre + tilt * h + sweep * e
            w = jnp.maximum(0.0, 1.0 - jnp.abs(pos - level))
            wgt[pl.ds(d * CHUNK + m * SHARE, SHARE), :] = w.astype(BF16)
    forward_marks()

    drain(mrcv.at[0], mr2)
    here = (iota((128, 128), 0) == s).astype(F32).astype(BF16)
    marks = jnp.dot(mrcv[...].reshape(2 * NS, 128), here, preferred_element_type=F32).astype(BF16)
    r = iota((K, 1), 0)
    a = r >> 2
    place = 96 * (a & 1) + 2 * (a >> 1) + ((r >> 1) & 1)
    twice = (place == iota((K, 2 * NS), 1)).astype(F32).astype(BF16)
    marks = jnp.dot(twice, marks, preferred_element_type=F32).astype(BF16)

    drain(rcv.at[pl.ds(0, NS - 1)], rs)
    rcv[pl.ds(s, 1)] = snd[pl.ds(s, 1)]
    both = jnp.concatenate([rcv[...].reshape(K, 128), marks], axis=1)
    diag = iota((128, 128), 0) == iota((128, 128), 1)

    def chunk(d):
        r = jnp.dot(wgt[pl.ds(pl.multiple_of(d * CHUNK, CHUNK), CHUNK), :], both, preferred_element_type=F32)
        ray = jnp.sum(jnp.where(diag, r[:, 128:], 0.0), axis=0, keepdims=True)
        return r[:, :128], ray

    for d in (4, 3, 5, 2, 6, 1, 7):
        t = (y + d) & 7
        num, ray = chunk(t)
        hi = ray.astype(BF16)
        lo = (ray - hi.astype(F32)).astype(BF16)
        part[t] = num.astype(BF16)
        hilo = jnp.concatenate([hi.astype(F32), lo.astype(F32)], axis=0)
        rpart[pl.ds(t, 1)] = hilo.astype(BF16).reshape(1, 2, 128)
        pltpu.make_async_remote_copy(
            src_ref=part.at[t], dst_ref=got.at[y], send_sem=ss2, recv_sem=rs2,
            device_id=(s, t), device_id_type=MESH,
        ).start()
        pltpu.make_async_remote_copy(
            src_ref=rpart.at[t], dst_ref=rgot.at[y], send_sem=ss3, recv_sem=rs3,
            device_id=(s, t), device_id_type=MESH,
        ).start()
    num, ray = chunk(y)
    got[pl.ds(y, 1)] = jnp.zeros((1, CHUNK, 128), BF16)
    rgot[pl.ds(y, 1)] = jnp.zeros((1, 2, 128), BF16)
    fetch[6].wait()
    drain(snd.at[pl.ds(0, NS - 1)], ss)
    drain(mrcv.at[0, pl.ds(0, 47)], ms)
    drain(mrcv.at[0], ms2)
    drain(rgot.at[pl.ds(0, NV - 1)], rs3)
    drain(got.at[pl.ds(0, NV - 1)], rs2)
    for v in range(NV):
        num = num + got[v].astype(F32)
        tail = rgot[v].astype(F32)
        ray = ray + (tail[0:1] + tail[1:2])
    rayc = jnp.broadcast_to(ray, (128, 128)).T
    new = RELAX * num / (rayc + SHIFT)
    upd[0:MB] = new.reshape(MB, SHARE, 128)
    upd[MB:MB + 1] = jnp.zeros((1, SHARE, 128), F32)
    for b in range(16):
        slot = jnp.int32(MB)
        for m in range(MB):
            slot = jnp.where(occ[0, m] == b, m, slot)
        out[b] = vol[b] + upd[slot]
    drain(part.at[pl.ds(0, NV - 1)], ss2)
    drain(rpart.at[pl.ds(0, NV - 1)], ss3)


def per_device(residual, route_list, tile_offsets, view_geometry, line_coords, occupied, volume):
    hbm = pl.BlockSpec(memory_space=pltpu.HBM)
    sem = pltpu.SemaphoreType.DMA
    return pl.pallas_call(
        body,
        out_shape=jax.ShapeDtypeStruct(volume.shape, F32),
        in_specs=[hbm] * 7,
        out_specs=pl.BlockSpec(memory_space=pltpu.VMEM),
        scratch_shapes=[
            pltpu.SMEM((VIEWS,), jnp.int32),
            pltpu.SMEM((1, MB), jnp.int32),
            pltpu.VMEM((384, 128), BF16),
            pltpu.VMEM((1, 2, NS), jnp.int32),
            pltpu.VMEM((4, VIEWS), F32),
            pltpu.VMEM((2, 16, 128), F32),
            pltpu.VMEM((16, SHARE, 128), F32),
            pltpu.VMEM((NS, ROWS, 128), BF16),
            pltpu.VMEM((NS, ROWS, 128), BF16),
            pltpu.VMEM((2, 48, 2, 128), BF16),
            pltpu.VMEM((NV * CHUNK, K), BF16),
            pltpu.VMEM((NV, CHUNK, 128), BF16),
            pltpu.VMEM((NV, CHUNK, 128), BF16),
            pltpu.VMEM((NV, 2, 128), BF16),
            pltpu.VMEM((NV, 2, 128), BF16),
            pltpu.VMEM((MB + 1, SHARE, 128), F32),
            sem((7,)), sem, sem, sem, sem, sem, sem, sem, sem, sem, sem,
        ],
        compiler_params=pltpu.CompilerParams(
            collective_id=0, has_side_effects=True, vmem_limit_bytes=60 << 20
        ),
    )(
        tile_offsets, occupied, residual.reshape(384, 128), jnp.swapaxes(route_list, 1, 2),
        view_geometry, line_coords, volume,
    )


def solution(mesh):
    placed = (
        P(("view", "slab"), None, None, None),
        P(("view", "slab"), None, None),
        P(),
        P(),
        P(None, "slab", None),
        P("slab", None),
        P("slab", "view", None),
    )
    return jax.shard_map(
        per_device, mesh=mesh, in_specs=placed, out_specs=P("slab", "view", None), check_vma=False
    )
```

```python
import jax
import jax.numpy as jnp
from jax import lax
from jax.experimental import pallas as pl
from jax.experimental.pallas import tpu as pltpu
from jax.sharding import PartitionSpec as P

MESH = pl.DeviceIdType.MESH
F32 = jnp.float32
BF16 = jnp.bfloat16

NS = 96
NV = 8
VIEWS = 768
ROWS = 4
K = NS * ROWS
MB = 8
SHARE = 16
CHUNK = MB * SHARE
RELAX = 0.9
SHIFT = 0.1 * VIEWS


def iota(shape, dim):
    return lax.broadcasted_iota(jnp.int32, shape, dim)


def drain(ref, sem):
    pltpu.make_async_copy(ref, ref, sem).wait()


def ring(v, step, n):
    t = v + step
    return jnp.where(t >= n, t - n, t)


def peers(s, act):
    x = s // 24
    z = (s - 24 * x) >> 1
    c = s & 1
    bases = [24 * ((x + dx) & 3) + (c ^ dc) for dx in (2, 1, 3, 0) for dc in (1, 0)]

    def column(i, carry):
        dz = 6 + ((i + 1) >> 1) * (1 - 2 * (i & 1))
        t = 2 * ring(z, dz, 12)
        for base in bases:
            act(base + t)
        return carry

    lax.fori_loop(0, 11, column, 0)
    for base in bases[:-1]:
        act(base + 2 * z)


def body(
    offs_h, occ_h, res_h, route_h, geo_h, lines_h, vol_h, out,
    offs, occ, res, route, geo, lines, vol,
    full, outs, snd, rcv, mrcv, wgt, part, got, rpart, rgot, upd, ins, ss, rs, ms, mr, ms2, mr2, ss2, rs2, ss3, rs3,
):
    s = lax.axis_index("slab")
    y = lax.axis_index("view")
    view = y * NS + s
    x = s // 24
    z = (s - 24 * x) >> 1
    core = s & 1
    k = 2 * x + core

    fetch = [
        pltpu.make_async_copy(h, v, ins.at[i])
        for i, (h, v) in enumerate(
            [
                (res_h, res), (route_h, route), (geo_h, geo), (offs_h, offs),
                (occ_h, occ), (lines_h, lines), (vol_h, vol),
            ]
        )
    ]
    for i in (1, 0, 2, 3, 4, 5, 6):
        fetch[i].start()

    bar = pltpu.get_barrier_semaphore()

    def greet(p):
        pl.semaphore_signal(bar, inc=1, device_id=(p, y), device_id_type=MESH)

    peers(s, greet)
    for d in range(1, NV):
        pl.semaphore_signal(bar, inc=1, device_id=(s, (y + d) & 7), device_id_type=MESH)

    fetch[1].wait()
    blocks = route[0].astype(F32)
    listed = blocks.astype(BF16)
    owner = (iota((K, NS), 0) >> 2) == iota((K, NS), 1)
    spread = lax.dot_general(
        owner.astype(F32).astype(BF16), listed, (((1,), (1,)), ((), ())), preferred_element_type=F32
    )
    q = iota((K, 1), 0) & 3
    block = jnp.where(q < 2, spread[:, 0:1], spread[:, 1:2])
    want = 2.0 * block + (q & 1).astype(F32)
    pick = (iota((K, 384), 1).astype(F32) == want).astype(F32).astype(BF16)
    flags = jnp.where(blocks >= 0.0, 1.0, 0.0)
    flags = jnp.concatenate([flags, jnp.zeros((2, 128 - NS), F32)], axis=1)
    mrcv[pl.ds(k, 1), pl.ds(z, 1)] = flags.astype(BF16).reshape(1, 1, 2, 128)

    fetch[2].wait()
    fetch[3].wait()
    g = geo[...]
    lane = iota((4, VIEWS), 1)
    mine = jnp.sum(jnp.where(lane == view, g, 0.0), axis=1, keepdims=True)
    slope = 0.8 + 0.05 * mine[3:4, :]
    off = offs[view].astype(F32)
    col = iota((128, 128), 0).astype(F32)
    xs = iota((128, 128), 1).astype(F32)
    table = jnp.maximum(0.0, 1.0 - jnp.abs(col - (off + slope * xs))).astype(BF16)
    fetch[0].wait()
    proj = jnp.dot(res[...], table, preferred_element_type=F32).astype(BF16)
    tile = jnp.dot(pick, proj, preferred_element_type=F32)
    snd[...] = tile.astype(BF16).reshape(NS, ROWS, 128)

    pl.semaphore_wait(bar, NS - 1 + NV - 1)

    def send_marks(i, c):
        dz = 6 + ((i + 1) >> 1) * (1 - 2 * (i & 1))
        t = ring(z, dz, 12)
        pltpu.make_async_remote_copy(
            src_ref=mrcv.at[k, z], dst_ref=mrcv.at[k, z], send_sem=ms, recv_sem=mr,
            device_id=(24 * x + 2 * t + core, y), device_id_type=MESH,
        ).start()
        return c

    lax.fori_loop(0, 11, send_marks, 0)

    def send(p):
        pltpu.make_async_remote_copy(
            src_ref=snd.at[p], dst_ref=rcv.at[s], send_sem=ss, recv_sem=rs,
            device_id=(p, y), device_id_type=MESH,
        ).start()

    peers(s, send)

    for f in fetch[4:6]:
        f.wait()
    g1 = g.astype(BF16)
    r1 = g - g1.astype(F32)
    g2 = r1.astype(BF16)
    g3 = (r1 - g2.astype(F32)).astype(BF16)
    sel = (iota((VIEWS, K), 0) - y * NS) == (iota((VIEWS, K), 1) >> 2)
    sel = sel.astype(F32).astype(BF16)
    gg = (
        jnp.dot(g1, sel, preferred_element_type=F32)
        + jnp.dot(g2, sel, preferred_element_type=F32)
        + jnp.dot(g3, sel, preferred_element_type=F32)
    )
    centre = 1.25 + 0.5 * gg[0:1]
    tilt = 0.6 + 0.6 * gg[1:2]
    sweep = 1.2 * gg[2:3] - 0.6
    level = (iota((1, K), 1) & 3).astype(F32)
    def forward_marks():
        drain(mrcv.at[0, pl.ds(0, 11)], mr)
        for dx, dc in ((2, 1), (2, 0), (1, 1), (3, 1), (1, 0), (3, 0), (0, 1)):
            p = 24 * ((x + dx) & 3) + 2 * z + (core ^ dc)
            pltpu.make_async_remote_copy(
                src_ref=mrcv.at[k], dst_ref=mrcv.at[k], send_sem=ms2, recv_sem=mr2,
                device_id=(p, y), device_id_type=MESH,
            ).start()

    hs = []
    ds = []
    for m in range(MB):
        brick = jnp.maximum(occ[0, m], 0)
        hs.append(3.0 * lines[0, pl.ds(brick, 1), :] - 1.5)
        ds.append(lines[1, pl.ds(brick, 1), :] - 0.5)
    hd = jnp.concatenate(hs + ds + [jnp.zeros((112, 128), F32)], axis=0)
    hdt = hd.T
    for d in range(NV):
        for m in range(MB):
            h = hdt[d * SHARE:(d + 1) * SHARE, m:m + 1]
            e = hdt[d * SHARE:(d + 1) * SHARE, MB + m:MB + m + 1]
            pos = centre + tilt * h + sweep * e
            w = jnp.maximum(0.0, 1.0 - jnp.abs(pos - level))
            wgt[pl.ds(d * CHUNK + m * SHARE, SHARE), :] = w.astype(BF16)
    forward_marks()

    slots = []
    for b in range(16):
        slot = jnp.int32(MB)
        for m in range(MB):
            slot = jnp.where(occ[0, m] == b, m, slot)
        slots.append(slot)

    drain(mrcv.at[pl.ds(0, 7)], mr2)
    here = (iota((128, 128), 0) == s).astype(F32).astype(BF16)
    marks = jnp.dot(mrcv[...].reshape(2 * NS, 128), here, preferred_element_type=F32).astype(BF16)
    r = iota((K, 1), 0)
    a = r >> 2
    xa = (a >= 24).astype(jnp.int32) + (a >= 48).astype(jnp.int32) + (a >= 72).astype(jnp.int32)
    place = 24 * (2 * xa + (a & 1)) + 2 * ((a - 24 * xa) >> 1) + ((r >> 1) & 1)
    twice = (place == iota((K, 2 * NS), 1)).astype(F32).astype(BF16)
    marks = jnp.dot(twice, marks, preferred_element_type=F32).astype(BF16)

    drain(rcv.at[pl.ds(0, NS - 1)], rs)
    rcv[pl.ds(s, 1)] = snd[pl.ds(s, 1)]
    both = jnp.concatenate([rcv[...].reshape(K, 128), marks], axis=1)
    diag = iota((128, 128), 0) == iota((128, 128), 1)

    def chunk(d):
        r = jnp.dot(wgt[pl.ds(pl.multiple_of(d * CHUNK, CHUNK), CHUNK), :], both, preferred_element_type=F32)
        ray = jnp.sum(jnp.where(diag, r[:, 128:], 0.0), axis=0, keepdims=True)
        return r[:, :128], ray

    for d in (4, 3, 5, 2, 6, 1, 7):
        t = (y + d) & 7
        num, ray = chunk(t)
        hi = ray.astype(BF16)
        lo = (ray - hi.astype(F32)).astype(BF16)
        part[t] = num.astype(BF16)
        hilo = jnp.concatenate([hi.astype(F32), lo.astype(F32)], axis=0)
        rpart[pl.ds(t, 1)] = hilo.astype(BF16).reshape(1, 2, 128)
        pltpu.make_async_remote_copy(
            src_ref=part.at[t], dst_ref=got.at[y], send_sem=ss2, recv_sem=rs2.at[y],
            device_id=(s, t), device_id_type=MESH,
        ).start()
        pltpu.make_async_remote_copy(
            src_ref=rpart.at[t], dst_ref=rgot.at[y], send_sem=ss3, recv_sem=rs3,
            device_id=(s, t), device_id_type=MESH,
        ).start()
    num, ray = chunk(y)
    rgot[pl.ds(y, 1)] = jnp.zeros((1, 2, 128), BF16)
    fetch[6].wait()
    drain(snd.at[pl.ds(0, NS - 1)], ss)
    drain(mrcv.at[0, pl.ds(0, 11)], ms)
    drain(mrcv.at[pl.ds(0, 7)], ms2)
    for d in (1, 7, 2, 6, 3, 5, 4):
        v = (y + d) & 7
        drain(got.at[v], rs2.at[v])
        num = num + got[v].astype(F32)
    drain(rgot.at[pl.ds(0, NV - 1)], rs3)
    for v in range(NV):
        tail = rgot[v].astype(F32)
        ray = ray + (tail[0:1] + tail[1:2])
    rayc = jnp.broadcast_to(ray, (128, 128)).T
    new = RELAX * num / (rayc + SHIFT)
    upd[0:MB] = new.reshape(MB, SHARE, 128)
    upd[MB:MB + 1] = jnp.zeros((1, SHARE, 128), F32)
    stores = []
    for b in range(16):
        full[b] = vol[b] + upd[slots[b]]
        if b % 4 == 3:
            span = pl.ds(b - 3, 4)
            stores.append(pltpu.make_async_copy(full.at[span], out.at[span], outs.at[b // 4]))
            stores[-1].start()
    drain(part.at[pl.ds(0, NV - 1)], ss2)
    drain(rpart.at[pl.ds(0, NV - 1)], ss3)
    for f in stores:
        f.wait()


def per_device(residual, route_list, tile_offsets, view_geometry, line_coords, occupied, volume):
    hbm = pl.BlockSpec(memory_space=pltpu.HBM)
    sem = pltpu.SemaphoreType.DMA
    return pl.pallas_call(
        body,
        out_shape=jax.ShapeDtypeStruct(volume.shape, F32),
        in_specs=[hbm] * 7,
        out_specs=hbm,
        scratch_shapes=[
            pltpu.SMEM((VIEWS,), jnp.int32),
            pltpu.SMEM((1, MB), jnp.int32),
            pltpu.VMEM((384, 128), BF16),
            pltpu.VMEM((1, 2, NS), jnp.int32),
            pltpu.VMEM((4, VIEWS), F32),
            pltpu.VMEM((2, 16, 128), F32),
            pltpu.VMEM((16, SHARE, 128), F32),
            pltpu.VMEM((16, SHARE, 128), F32),
            sem((4,)),
            pltpu.VMEM((NS, ROWS, 128), BF16),
            pltpu.VMEM((NS, ROWS, 128), BF16),
            pltpu.VMEM((8, 12, 2, 128), BF16),
            pltpu.VMEM((NV * CHUNK, K), BF16),
            pltpu.VMEM((NV, CHUNK, 128), BF16),
            pltpu.VMEM((NV, CHUNK, 128), BF16),
            pltpu.VMEM((NV, 2, 128), BF16),
            pltpu.VMEM((NV, 2, 128), BF16),
            pltpu.VMEM((MB + 1, SHARE, 128), F32),
            sem((7,)), sem, sem, sem, sem, sem, sem, sem, sem((NV,)), sem, sem,
        ],
        compiler_params=pltpu.CompilerParams(
            collective_id=0, has_side_effects=True, vmem_limit_bytes=60 << 20
        ),
    )(
        tile_offsets, occupied, residual.reshape(384, 128), jnp.swapaxes(route_list, 1, 2),
        view_geometry, line_coords, volume,
    )


def solution(mesh):
    placed = (
        P(("view", "slab"), None, None, None),
        P(("view", "slab"), None, None),
        P(),
        P(),
        P(None, "slab", None),
        P("slab", None),
        P("slab", "view", None),
    )
    return jax.shard_map(
        per_device, mesh=mesh, in_specs=placed, out_specs=P("slab", "view", None), check_vma=False
    )
```

```python
import jax
import jax.numpy as jnp
from jax import lax
from jax.experimental import pallas as pl
from jax.experimental.pallas import tpu as pltpu
from jax.sharding import PartitionSpec as P

MESH = pl.DeviceIdType.MESH
F32 = jnp.float32
BF16 = jnp.bfloat16

NS = 96
NV = 8
VIEWS = 768
ROWS = 4
K = NS * ROWS
MB = 8
SHARE = 16
CHUNK = MB * SHARE
RELAX = 0.9
SHIFT = 0.1 * VIEWS


def iota(shape, dim):
    return lax.broadcasted_iota(jnp.int32, shape, dim)


def drain(ref, sem):
    pltpu.make_async_copy(ref, ref, sem).wait()


def ring(v, step, n):
    t = v + step
    return jnp.where(t >= n, t - n, t)


def peers(s, act):
    x = s // 24
    z = (s - 24 * x) >> 1
    c = s & 1
    bases = [24 * ((x + dx) & 3) + (c ^ dc) for dx in (2, 1, 3, 0) for dc in (1, 0)]

    def column(i, carry):
        dz = 6 + ((i + 1) >> 1) * (1 - 2 * (i & 1))
        t = 2 * ring(z, dz, 12)
        for base in bases:
            act(base + t)
        return carry

    lax.fori_loop(0, 11, column, 0)
    for base in bases[:-1]:
        act(base + 2 * z)


def body(
    offs_h, occ_h, res_h, route_h, geo_h, lines_h, vol_h, out,
    offs, occ, res, route, geo, lines, vol,
    snd, rcv, mrcv, wgt, part, got, rpart, rgot, upd, ins, ss, rs, ms, mr, ms2, mr2, ss2, rs2, ss3, rs3,
):
    s = lax.axis_index("slab")
    y = lax.axis_index("view")
    view = y * NS + s
    x = s // 24
    z = (s - 24 * x) >> 1
    core = s & 1
    k = 2 * x + core

    fetch = [
        pltpu.make_async_copy(h, v, ins.at[i])
        for i, (h, v) in enumerate(
            [
                (res_h, res), (route_h, route), (geo_h, geo), (offs_h, offs),
                (occ_h, occ), (lines_h, lines), (vol_h, vol),
            ]
        )
    ]
    for f in fetch:
        f.start()

    bar = pltpu.get_barrier_semaphore()

    def greet(p):
        pl.semaphore_signal(bar, inc=1, device_id=(p, y), device_id_type=MESH)

    peers(s, greet)
    for d in range(1, NV):
        pl.semaphore_signal(bar, inc=1, device_id=(s, (y + d) & 7), device_id_type=MESH)

    for f in fetch[:4]:
        f.wait()
    g = geo[...]
    lane = iota((4, VIEWS), 1)
    mine = jnp.sum(jnp.where(lane == view, g, 0.0), axis=1, keepdims=True)
    slope = 0.8 + 0.05 * mine[3:4, :]
    off = offs[view].astype(F32)
    col = iota((128, 128), 0).astype(F32)
    xs = iota((128, 128), 1).astype(F32)
    table = jnp.maximum(0.0, 1.0 - jnp.abs(col - (off + slope * xs))).astype(BF16)
    proj = jnp.dot(res[...], table, preferred_element_type=F32).astype(BF16)

    blocks = route[0].astype(F32)
    listed = blocks.astype(BF16)
    owner = (iota((K, NS), 0) >> 2) == iota((K, NS), 1)
    spread = lax.dot_general(
        owner.astype(F32).astype(BF16), listed, (((1,), (1,)), ((), ())), preferred_element_type=F32
    )
    q = iota((K, 1), 0) & 3
    block = jnp.where(q < 2, spread[:, 0:1], spread[:, 1:2])
    want = 2.0 * block + (q & 1).astype(F32)
    pick = (iota((K, 384), 1).astype(F32) == want).astype(F32).astype(BF16)
    tile = jnp.dot(pick, proj, preferred_element_type=F32)
    snd[...] = tile.astype(BF16).reshape(NS, ROWS, 128)
    flags = jnp.where(blocks >= 0.0, 1.0, 0.0)
    flags = jnp.concatenate([flags, jnp.zeros((2, 128 - NS), F32)], axis=1)
    mrcv[pl.ds(k, 1), pl.ds(z, 1)] = flags.astype(BF16).reshape(1, 1, 2, 128)

    pl.semaphore_wait(bar, NS - 1 + NV - 1)

    def send_marks(i, c):
        dz = 6 + ((i + 1) >> 1) * (1 - 2 * (i & 1))
        t = ring(z, dz, 12)
        pltpu.make_async_remote_copy(
            src_ref=mrcv.at[k, z], dst_ref=mrcv.at[k, z], send_sem=ms, recv_sem=mr,
            device_id=(24 * x + 2 * t + core, y), device_id_type=MESH,
        ).start()
        return c

    lax.fori_loop(0, 11, send_marks, 0)

    def send(p):
        pltpu.make_async_remote_copy(
            src_ref=snd.at[p], dst_ref=rcv.at[s], send_sem=ss, recv_sem=rs,
            device_id=(p, y), device_id_type=MESH,
        ).start()

    peers(s, send)

    for f in fetch[4:6]:
        f.wait()
    g1 = g.astype(BF16)
    r1 = g - g1.astype(F32)
    g2 = r1.astype(BF16)
    g3 = (r1 - g2.astype(F32)).astype(BF16)
    sel = (iota((VIEWS, K), 0) - y * NS) == (iota((VIEWS, K), 1) >> 2)
    sel = sel.astype(F32).astype(BF16)
    gg = (
        jnp.dot(g1, sel, preferred_element_type=F32)
        + jnp.dot(g2, sel, preferred_element_type=F32)
        + jnp.dot(g3, sel, preferred_element_type=F32)
    )
    centre = 1.25 + 0.5 * gg[0:1]
    tilt = 0.6 + 0.6 * gg[1:2]
    sweep = 1.2 * gg[2:3] - 0.6
    level = (iota((1, K), 1) & 3).astype(F32)
    def forward_marks():
        drain(mrcv.at[0, pl.ds(0, 11)], mr)
        for dx, dc in ((2, 1), (2, 0), (1, 1), (3, 1), (1, 0), (3, 0), (0, 1)):
            p = 24 * ((x + dx) & 3) + 2 * z + (core ^ dc)
            pltpu.make_async_remote_copy(
                src_ref=mrcv.at[k], dst_ref=mrcv.at[k], send_sem=ms2, recv_sem=mr2,
                device_id=(p, y), device_id_type=MESH,
            ).start()

    hs = []
    ds = []
    for m in range(MB):
        brick = jnp.maximum(occ[0, m], 0)
        hs.append(3.0 * lines[0, pl.ds(brick, 1), :] - 1.5)
        ds.append(lines[1, pl.ds(brick, 1), :] - 0.5)
    hd = jnp.concatenate(hs + ds + [jnp.zeros((112, 128), F32)], axis=0)
    hdt = hd.T
    for d in range(NV):
        for m in range(MB):
            h = hdt[d * SHARE:(d + 1) * SHARE, m:m + 1]
            e = hdt[d * SHARE:(d + 1) * SHARE, MB + m:MB + m + 1]
            pos = centre + tilt * h + sweep * e
            w = jnp.maximum(0.0, 1.0 - jnp.abs(pos - level))
            wgt[pl.ds(d * CHUNK + m * SHARE, SHARE), :] = w.astype(BF16)
    forward_marks()

    drain(mrcv.at[pl.ds(0, 7)], mr2)
    here = (iota((128, 128), 0) == s).astype(F32).astype(BF16)
    marks = jnp.dot(mrcv[...].reshape(2 * NS, 128), here, preferred_element_type=F32).astype(BF16)
    r = iota((K, 1), 0)
    a = r >> 2
    xa = (a >= 24).astype(jnp.int32) + (a >= 48).astype(jnp.int32) + (a >= 72).astype(jnp.int32)
    place = 24 * (2 * xa + (a & 1)) + 2 * ((a - 24 * xa) >> 1) + ((r >> 1) & 1)
    twice = (place == iota((K, 2 * NS), 1)).astype(F32).astype(BF16)
    marks = jnp.dot(twice, marks, preferred_element_type=F32).astype(BF16)

    drain(rcv.at[pl.ds(0, NS - 1)], rs)
    rcv[pl.ds(s, 1)] = snd[pl.ds(s, 1)]
    both = jnp.concatenate([rcv[...].reshape(K, 128), marks], axis=1)
    diag = iota((128, 128), 0) == iota((128, 128), 1)

    def chunk(d):
        r = jnp.dot(wgt[pl.ds(pl.multiple_of(d * CHUNK, CHUNK), CHUNK), :], both, preferred_element_type=F32)
        ray = jnp.sum(jnp.where(diag, r[:, 128:], 0.0), axis=0, keepdims=True)
        return r[:, :128], ray

    for d in (4, 3, 5, 2, 6, 1, 7):
        t = (y + d) & 7
        num, ray = chunk(t)
        hi = ray.astype(BF16)
        lo = (ray - hi.astype(F32)).astype(BF16)
        part[t] = num.astype(BF16)
        hilo = jnp.concatenate([hi.astype(F32), lo.astype(F32)], axis=0)
        rpart[pl.ds(t, 1)] = hilo.astype(BF16).reshape(1, 2, 128)
        pltpu.make_async_remote_copy(
            src_ref=part.at[t], dst_ref=got.at[y], send_sem=ss2, recv_sem=rs2,
            device_id=(s, t), device_id_type=MESH,
        ).start()
        pltpu.make_async_remote_copy(
            src_ref=rpart.at[t], dst_ref=rgot.at[y], send_sem=ss3, recv_sem=rs3,
            device_id=(s, t), device_id_type=MESH,
        ).start()
    num, ray = chunk(y)
    got[pl.ds(y, 1)] = jnp.zeros((1, CHUNK, 128), BF16)
    rgot[pl.ds(y, 1)] = jnp.zeros((1, 2, 128), BF16)
    fetch[6].wait()
    drain(snd.at[pl.ds(0, NS - 1)], ss)
    drain(mrcv.at[0, pl.ds(0, 11)], ms)
    drain(mrcv.at[pl.ds(0, 7)], ms2)
    drain(rgot.at[pl.ds(0, NV - 1)], rs3)
    drain(got.at[pl.ds(0, NV - 1)], rs2)
    for v in range(NV):
        num = num + got[v].astype(F32)
        tail = rgot[v].astype(F32)
        ray = ray + (tail[0:1] + tail[1:2])
    rayc = jnp.broadcast_to(ray, (128, 128)).T
    new = RELAX * num / (rayc + SHIFT)
    upd[0:MB] = new.reshape(MB, SHARE, 128)
    upd[MB:MB + 1] = jnp.zeros((1, SHARE, 128), F32)
    for b in range(16):
        slot = jnp.int32(MB)
        for m in range(MB):
            slot = jnp.where(occ[0, m] == b, m, slot)
        out[b] = vol[b] + upd[slot]
    drain(part.at[pl.ds(0, NV - 1)], ss2)
    drain(rpart.at[pl.ds(0, NV - 1)], ss3)


def per_device(residual, route_list, tile_offsets, view_geometry, line_coords, occupied, volume):
    hbm = pl.BlockSpec(memory_space=pltpu.HBM)
    sem = pltpu.SemaphoreType.DMA
    return pl.pallas_call(
        body,
        out_shape=jax.ShapeDtypeStruct(volume.shape, F32),
        in_specs=[hbm] * 7,
        out_specs=pl.BlockSpec(memory_space=pltpu.VMEM),
        scratch_shapes=[
            pltpu.SMEM((VIEWS,), jnp.int32),
            pltpu.SMEM((1, MB), jnp.int32),
            pltpu.VMEM((384, 128), BF16),
            pltpu.VMEM((1, 2, NS), jnp.int32),
            pltpu.VMEM((4, VIEWS), F32),
            pltpu.VMEM((2, 16, 128), F32),
            pltpu.VMEM((16, SHARE, 128), F32),
            pltpu.VMEM((NS, ROWS, 128), BF16),
            pltpu.VMEM((NS, ROWS, 128), BF16),
            pltpu.VMEM((8, 12, 2, 128), BF16),
            pltpu.VMEM((NV * CHUNK, K), BF16),
            pltpu.VMEM((NV, CHUNK, 128), BF16),
            pltpu.VMEM((NV, CHUNK, 128), BF16),
            pltpu.VMEM((NV, 2, 128), BF16),
            pltpu.VMEM((NV, 2, 128), BF16),
            pltpu.VMEM((MB + 1, SHARE, 128), F32),
            sem((7,)), sem, sem, sem, sem, sem, sem, sem, sem, sem, sem,
        ],
        compiler_params=pltpu.CompilerParams(
            collective_id=0, has_side_effects=True, vmem_limit_bytes=60 << 20
        ),
    )(
        tile_offsets, occupied, residual.reshape(384, 128), jnp.swapaxes(route_list, 1, 2),
        view_geometry, line_coords, volume,
    )


def solution(mesh):
    placed = (
        P(("view", "slab"), None, None, None),
        P(("view", "slab"), None, None),
        P(),
        P(),
        P(None, "slab", None),
        P("slab", None),
        P("slab", "view", None),
    )
    return jax.shard_map(
        per_device, mesh=mesh, in_specs=placed, out_specs=P("slab", "view", None), check_vma=False
    )
```
